32 devices in a mesh: ha: 8 (over z, y), vert: 4 (over x, core).
Axes of the slice: x: 2, y: 2, z: 4, core: 2. Of those that a mesh axis runs over, the one named last changes fastest.
Arguments:
- rhs: float32 [256, 32, 256], P('vert', 'ha'), may hold values from -4 to 4
- guess: float32 [256, 32, 256], P('vert', 'ha'), may hold values from -6 to 6
- vertical_coupling: float32 [256, 32, 256], P('vert', 'ha'), may hold values from 5 to 2500
- lateral_coupling: float32 [256, 32, 256], P('vert', 'ha'), may hold values from 0.25 to 1
Outputs:
- smoothed: float32 [256, 32, 256], P('vert', 'ha')
- coarse_residual: float32 [128, 32, 256], P('vert', 'ha')
The draws below stay inside these ranges and needn't reach their ends.
All inputs are finite; a program needn't handle non-finite values.
Results may differ from the reference program's by a relative error of at most 0.0007.
Values sent between devices are 32-bit elements; how exact they have to be, the bound alone decides.
A program may use at most 128 MiB of HBM per device.

```python
import math
import jax
import jax.numpy as jnp
from jax import lax

NY = 256
SWEEPS = 2
NX = 32
NZ = 256


def draw_rhs(key, part):
    base_key = jax.random.fold_in(key, 11)
    return jax.random.truncated_normal(base_key, -4.0, 4.0, (NZ, NX, NY), jnp.float32)


def draw_vertical_coupling(key, part):
    column_key = jax.random.fold_in(key, 21)
    cell_key = jax.random.fold_in(key, 22)
    strength = jnp.exp(jax.random.uniform(column_key, (NX, NY), jnp.float32, math.log(5.0), math.log(1000.0)))
    factor = jax.random.uniform(cell_key, (NZ, NX, NY), jnp.float32, 1.0, 2.5)
    return strength[None] * factor


def levels(own_key, extent, split, least, high):
    def one(axis_at, blocks):
        steps = jax.random.uniform(jax.random.fold_in(jax.random.fold_in(own_key, 6), axis_at), (blocks,), jnp.float32, least / len(split), high / len(split))
        return jnp.repeat(jnp.exp(steps), extent[axis_at] // blocks).reshape((-1,) + (1,) * (len(extent) - axis_at - 1))

    level = one(*split[0])
    for cut in split[1:]:
        level = level * one(*cut)
    return level


def noise(own_key, extent, scale, reach, split=(), dtype=jnp.bfloat16):
    gain = levels(own_key, extent, split, -0.22, 0.18) if split else 1.0
    drawn = jax.random.normal(own_key, extent, jnp.float32) * scale * gain
    return jnp.minimum(jnp.maximum(drawn, -reach), reach).astype(dtype)


def setup_inputs(seed: int = 0) -> dict:
    keys = jax.random.split(jax.random.key(seed), 5)
    return {
        "rhs": draw_rhs(jax.random.fold_in(keys[4], 71), 0),
        "guess": noise(keys[1], (NZ, NX, NY), 1.0, 6.0, ((0, 4), (1, 8)), jnp.float32),
        "vertical_coupling": draw_vertical_coupling(jax.random.fold_in(keys[4], 71), 0),
        "lateral_coupling": jnp.clip(jnp.exp(math.log(1.0) - 1.3862944 * jax.random.uniform(keys[3], (NZ, NX, NY), jnp.float32) ** levels(keys[3], (NZ, NX, NY), ((0, 4), (1, 8)), -0.2, 0.2)), 0.25, 1.0),
    }


def lateral_sum(field):
    padded = jnp.pad(field, ((0, 0), (1, 1), (1, 1)))
    return padded[:, :-2, 1:-1] + padded[:, 2:, 1:-1] + padded[:, 1:-1, :-2] + padded[:, 1:-1, 2:]


def tridiagonal(lower_k, center_k, upper_k, source):
    blank = jnp.zeros(source.shape[1:], jnp.float32)

    def forward(state_pair, level_row):
        pivot_prev, value_prev = state_pair
        coef_low, coef_mid, coef_up, right_val = level_row
        divisor = coef_mid - coef_low * pivot_prev
        pivot = coef_up / divisor
        value = (right_val + coef_low * value_prev) / divisor
        return (pivot, value), (pivot, value)

    _, (pivots, values) = lax.scan(forward, (blank, blank), (lower_k, center_k, upper_k, source))

    def backward(next_value, level_row):
        pivot, value = level_row
        result = value + pivot * next_value
        return result, result

    _, solved = lax.scan(backward, blank, (pivots, values), reverse=True)
    return solved


def reference(rhs, guess, vertical_coupling, lateral_coupling):
    lowest = jnp.zeros_like(vertical_coupling[:1])
    below_coupling = jnp.concatenate([lowest, vertical_coupling[:-1]], 0)
    diagonal = 4.0 * lateral_coupling + vertical_coupling + below_coupling
    index_x = jnp.arange(NX)[:, None]
    index_y = jnp.arange(NY)[None, :]
    is_red = (index_x + index_y) % 2 == 0
    current = guess
    for sweep_no in range(SWEEPS):
        for colour_mask in (is_red, jnp.logical_not(is_red)):
            source = rhs + lateral_coupling * lateral_sum(current)
            solved = tridiagonal(below_coupling, diagonal, vertical_coupling, source)
            current = jnp.where(colour_mask[None], solved, current)
    padded_z = jnp.pad(current, ((1, 1), (0, 0), (0, 0)))
    applied = diagonal * current - lateral_coupling * lateral_sum(current) - vertical_coupling * padded_z[2:] - below_coupling * padded_z[:-2]
    residual = rhs - applied
    with_rims = jnp.pad(residual, ((1, 1), (0, 0), (0, 0)))
    coarse = (with_rims[0:NZ:2] + 3.0 * with_rims[1:NZ + 1:2] + 3.0 * with_rims[2:NZ + 2:2] + with_rims[3:NZ + 3:2]) / 8.0
    return current, coarse
```

```python
import functools

import jax
import jax.numpy as jnp
from jax import lax
from jax.experimental import pallas as pl
from jax.experimental.pallas import tpu as pltpu
from jax.sharding import PartitionSpec as P

SWEEPS = 2
MESH = pl.DeviceIdType.MESH
LANES = 128


def kernel(
    depth, width, rhs, guess, up, lat, out, coarse,
    inv, fwd, bwd, first_g, last_g, src, work, res,
    low_in, pack, halo, ends0, ends, coef, edge_out, edge_in,
    low_send, low_recv, halo_send, halo_recv, end_send, end_recv, edge_send, edge_recv,
):
    levels = rhs.shape[0]
    rows = 4
    half = levels // 2
    chunk = levels // 8
    ha, vert = lax.axis_index("ha"), lax.axis_index("vert")
    sub = lax.broadcasted_iota(jnp.int32, (8, LANES), 0)
    lane = lax.broadcasted_iota(jnp.int32, (8, LANES), 1)
    row = sub % rows
    red = (row + lane) % 2 == 0
    zero = jnp.zeros((8, LANES), jnp.float32)

    def roll(a, by, axis):
        by = by % a.shape[axis]
        return a if by == 0 else pltpu.roll(a, by, axis)

    peers = [lax.rem(vert + o, depth) for o in range(1, depth)]
    barrier = pltpu.get_barrier_semaphore()
    for peer in peers:
        pl.semaphore_signal(barrier, inc=1, device_id=(ha, peer), device_id_type=MESH)

    @pl.when(ha > 0)
    def _():
        pl.semaphore_signal(barrier, inc=1, device_id=(ha - 1, vert), device_id_type=MESH)

    @pl.when(ha < width - 1)
    def _():
        pl.semaphore_signal(barrier, inc=1, device_id=(ha + 1, vert), device_id_type=MESH)

    def packed(acc, low_part, high_part, t, colour):
        result = []
        for side, from_row in ((0, rows - 1), (1, 0)):
            odd = (from_row + colour) % 2
            both = jnp.where(
                (lane % 2 == odd)[None], low_part, roll(high_part, -1 if odd else 1, 2)
            )
            both = roll(both, t - from_row, 1)
            result.append(both if acc is None else jnp.where((row == t)[None], both, acc[side]))
        return result

    def halo_copy(event, side):
        target = ha + 1 if side == 0 else ha - 1
        return pltpu.make_async_remote_copy(
            src_ref=pack.at[event, side], dst_ref=halo.at[event, side],
            send_sem=halo_send.at[event, side], recv_sem=halo_recv.at[event, side],
            device_id=(target, vert), device_id_type=MESH,
        )

    def halo_start(event, acc):
        pack[event, 0] = acc[0]
        pack[event, 1] = acc[1]

        @pl.when(ha < width - 1)
        def _():
            halo_copy(event, 0).start()

        @pl.when(ha > 0)
        def _():
            halo_copy(event, 1).start()

    def halo_wait(event):
        @pl.when(ha > 0)
        def _():
            halo_copy(event, 0).wait_recv()

        @pl.when(ha < width - 1)
        def _():
            halo_copy(event, 1).wait_recv()

    def unpacked(event, colour, t):
        lows, highs = [], []
        for side, from_row, to_row in ((0, rows - 1, 0), (1, 0, rows - 1)):
            odd = (from_row + colour) % 2
            both = roll(halo[event, side], to_row - t, 1)
            lows.append(both)
            highs.append(roll(both, 1 if odd else -1, 2))
        below, above = (row == 0)[None], (row == rows - 1)[None]
        return [
            jnp.where(below, pair[0], jnp.where(above, pair[1], 0.0)) for pair in (lows, highs)
        ]

    def lateral_inner(v):
        left = roll(v, 1, 2)
        right = roll(v, -1, 2)
        left = jnp.where(
            (lane == 0)[None], jnp.where((sub < rows)[None], 0.0, roll(left, rows, 1)), left
        )
        right = jnp.where(
            (lane == LANES - 1)[None], jnp.where((sub < rows)[None], roll(right, rows, 1), 0.0),
            right,
        )
        below = jnp.where((row == 0)[None], 0.0, roll(v, 1, 1))
        above = jnp.where((row == rows - 1)[None], 0.0, roll(v, -1, 1))
        return left + right + below + above

    def part(t):
        return pl.ds(t * chunk, chunk)

    def end_copy(event, buffer, slot, peer):
        return pltpu.make_async_remote_copy(
            src_ref=buffer.at[slot], dst_ref=buffer.at[slot],
            send_sem=end_send.at[event, peer], recv_sem=end_recv.at[event, slot],
            device_id=(ha, peer), device_id_type=MESH,
        )

    def end_buffer(event):
        return ends0 if event == 0 else ends.at[event - 1]

    def low_copy():
        return pltpu.make_async_remote_copy(
            src_ref=up.at[levels - 1], dst_ref=low_in, send_sem=low_send, recv_sem=low_recv,
            device_id=(ha, vert + 1), device_id_type=MESH,
        )

    def edge_copy(side):
        target = vert + 1 if side == 0 else vert - 1
        return pltpu.make_async_remote_copy(
            src_ref=edge_out.at[side], dst_ref=edge_in.at[side],
            send_sem=edge_send.at[side], recv_sem=edge_recv.at[side],
            device_id=(ha, target), device_id_type=MESH,
        )

    @pl.when(ha == 0)
    def _():
        for event in range(2 * SWEEPS + 1):
            halo[event, 0] = jnp.zeros(halo.shape[2:], jnp.float32)

    @pl.when(ha == width - 1)
    def _():
        for event in range(2 * SWEEPS + 1):
            halo[event, 1] = jnp.zeros(halo.shape[2:], jnp.float32)

    @pl.when(vert == 0)
    def _():
        low_in[...] = zero
        edge_in[0] = zero

    @pl.when(vert == depth - 1)
    def _():
        edge_in[1] = zero

    acc = None
    for t in range(4):
        acc = packed(acc, guess[part(t)], guess[part(t + 4)], t, 1)

    greeted = (ha > 0).astype(jnp.int32) + (ha < width - 1).astype(jnp.int32)
    pl.semaphore_wait(barrier, depth - 1 + greeted)

    @pl.when(vert < depth - 1)
    def _():
        low_copy().start()

    halo_start(0, acc)

    def partial_source(field):
        def body(t, carry):
            at = pl.ds(pl.multiple_of(t * chunk, chunk), chunk)
            src[at] = rhs[at] + lat[at] * lateral_inner(field[at])
            return carry
        lax.fori_loop(0, 8, body, 0, unroll=True)

    partial_source(guess)

    @pl.when(vert > 0)
    def _():
        low_copy().wait_recv()

    low0 = low_in[...]
    top = levels - 1
    up_top = up[top]

    def eliminate(k, carry, start):
        piv_l, g_l, piv_u, g_u = carry
        j = top - k
        low_k = low0 if start else up[k - 1]
        up_k = up[k]
        inv_k = 1.0 / (4.0 * lat[k] + up_k + low_k - low_k * piv_l)
        piv_l = up_k * inv_k
        g_l = inv_k if start else low_k * inv_k * g_l
        inv[k] = inv_k
        fwd[k] = low_k * inv_k
        bwd[k] = piv_l
        first_g[k] = g_l
        low_j, up_j = up[j - 1], up[j]
        inv_j = 1.0 / (4.0 * lat[j] + up_j + low_j - up_j * piv_u)
        piv_u = low_j * inv_j
        g_u = inv_j if start else up_j * inv_j * g_u
        inv[j] = inv_j
        fwd[j] = up_j * inv_j
        bwd[j] = piv_u
        last_g[j] = g_u
        return piv_l, g_l, piv_u, g_u

    carry = eliminate(0, (zero, zero, zero, zero), True)
    carry = lax.fori_loop(1, half, lambda k, c: eliminate(k, c, False), carry, unroll=True)
    piv_l, g_l, piv_u, g_u = carry
    meet = 1.0 / (1.0 - piv_l * piv_u)
    fa = g_l * meet
    fb = piv_u * fa
    lb = g_u * meet
    la = piv_l * lb
    first_g[half - 1] = fa
    first_g[half] = fb
    last_g[half] = lb
    last_g[half - 1] = la

    def respond(i, carry):
        fa, la, fb, lb = carry
        k = half - 1 - i
        j = half + i
        bk, bj = bwd[k], bwd[j]
        fa = first_g[k] + bk * fa
        la = bk * la
        fb = bj * fb
        lb = last_g[j] + bj * lb
        first_g[k] = fa
        last_g[k] = la
        first_g[j] = fb
        last_g[j] = lb
        return fa, la, fb, lb

    fa, la, fb, lb = lax.fori_loop(1, half, respond, (fa, la, fb, lb), unroll=True)
    own = [low0 * fa, low0 * fb, up_top * la, up_top * lb]

    def interface_coefficients():
        table = [[ends0[e, 2 + i] for i in range(4)] for e in range(depth)]
        slope_b, slope_a = zero, zero
        below = [zero] * (2 * depth)
        above = [zero] * (2 * depth)
        for e in range(depth - 1):
            v_f, v_l, w_f, w_l = table[e]
            keep = (e < vert).astype(jnp.float32)
            ratio = v_l * slope_b / (1.0 - v_f * slope_b)
            gain = keep * (v_l + ratio * v_f) + (1.0 - keep)
            below = [gain * b if n < 2 * e else b for n, b in enumerate(below)]
            below[2 * e] = keep * ratio
            below[2 * e + 1] = jnp.full((8, LANES), keep)
            slope_b = keep * (w_l + ratio * w_f) + (1.0 - keep) * slope_b
        for e in range(depth - 1, 0, -1):
            v_f, v_l, w_f, w_l = table[e]
            keep = (e > vert).astype(jnp.float32)
            ratio = w_f * slope_a / (1.0 - w_l * slope_a)
            gain = keep * (w_f + ratio * w_l) + (1.0 - keep)
            above = [gain * a if n > 2 * e + 1 else a for n, a in enumerate(above)]
            above[2 * e] = jnp.full((8, LANES), keep)
            above[2 * e + 1] = keep * ratio
            slope_a = keep * (v_f + ratio * v_l) + (1.0 - keep) * slope_a
        v_f, v_l, w_f, w_l = own
        c_ss, c_tt = 1.0 - slope_b * v_f, 1.0 - slope_a * w_l
        c_st, c_ts = slope_b * w_f, slope_a * v_l
        scale = 1.0 / (c_ss * c_tt - c_st * c_ts)
        for n in range(2 * depth):
            mine = (vert == n // 2).astype(jnp.float32)
            r_b = below[n] + mine * slope_b if n % 2 == 0 else below[n]
            r_a = above[n] + mine * slope_a if n % 2 == 1 else above[n]
            coef[0, n] = low0 * scale * (r_b * c_tt + c_st * r_a)
            coef[1, n] = up_top * scale * (c_ss * r_a + c_ts * r_b)

    reach = {}
    for event in range(2 * SWEEPS):
        colour = event % 2
        chosen = red if colour == 0 else jnp.logical_not(red)
        halo_wait(event)
        dot_f, dot_l = zero, zero
        for t in range(4):
            for where, outer in zip((part(t), part(t + 4)), unpacked(event, 1 - colour, t)):
                full = src[where] + lat[where] * outer
                src[where] = full
                dot_f = dot_f + jnp.sum(full * first_g[where], axis=0)
                dot_l = dot_l + jnp.sum(full * last_g[where], axis=0)
        buffer = end_buffer(event)
        buffer[vert, 0] = dot_f
        buffer[vert, 1] = dot_l
        if event == 0:
            for i in range(4):
                buffer[vert, 2 + i] = own[i]
        for peer in peers:
            end_copy(event, buffer, vert, peer).start()

        def forward(k, carry):
            f_l, f_u = carry
            j = top - k
            f_l = src[k] * inv[k] + fwd[k] * f_l
            f_u = src[j] * inv[j] + fwd[j] * f_u
            work[k] = f_l
            work[j] = f_u
            return f_l, f_u

        f_l, f_u = lax.fori_loop(0, half, forward, (zero, zero), unroll=True)
        y_l = (f_l + piv_l * f_u) * meet
        y_u = f_u + piv_u * y_l
        work[half - 1] = y_l
        work[half] = y_u

        def backward(i, carry):
            y_l, y_u = carry
            k = half - 1 - i
            j = half + i
            y_l = work[k] + bwd[k] * y_l
            y_u = work[j] + bwd[j] * y_u
            work[k] = y_l
            work[j] = y_u
            return y_l, y_u

        lax.fori_loop(1, half, backward, (y_l, y_u), unroll=True)
        for peer in peers:
            end_copy(event, buffer, peer, peer).wait_recv()
        if event == 0:
            interface_coefficients()
        from_b, from_a = zero, zero
        for n in range(2 * depth):
            value = buffer[n // 2, n % 2]
            from_b = from_b + coef[0, n] * value
            from_a = from_a + coef[1, n] * value
        reach[colour] = (from_b, from_a)
        old = guess if event == 0 else out
        acc = None
        for t in range(4):
            pair = []
            for where in (part(t), part(t + 4)):
                new = work[where] + first_g[where] * from_b + last_g[where] * from_a
                new = jnp.where(chosen[None], new, old[where])
                out[where] = new
                pair.append(new)
            acc = packed(acc, pair[0], pair[1], t, colour)
        halo_start(event + 1, acc)
        if event == 2 * SWEEPS - 1:
            def keep_source(t, carry):
                at = pl.ds(pl.multiple_of(t * chunk, chunk), chunk)
                inner = rhs[at] + lat[at] * lateral_inner(out[at])
                src[at] = jnp.where(red[None], inner, src[at])
                return carry
            lax.fori_loop(0, 8, keep_source, 0, unroll=True)
        else:
            partial_source(out)

    from_b = jnp.where(red, reach[0][0], reach[1][0])
    from_a = jnp.where(red, reach[0][1], reach[1][1])

    def applied(k):
        low_k = low0 if k == 0 else up[k - 1]
        under = from_b if k == 0 else low_k * out[k - 1]
        over = from_a if k == top else up[k] * out[k + 1]
        return (4.0 * lat[k] + up[k] + low_k) * out[k] - over - under

    res[0] = src[0] - applied(0)
    res[top] = src[top] - applied(top)

    def inner_level(k, carry):
        low_k, up_k = up[k - 1], up[k]
        res[k] = src[k] - (
            (4.0 * lat[k] + up_k + low_k) * out[k] - up_k * out[k + 1] - low_k * out[k - 1]
        )
        return carry

    lax.fori_loop(1, top, inner_level, 0, unroll=True)
    halo_wait(2 * SWEEPS)
    for t in range(4):
        for where, outer in zip((part(t), part(t + 4)), unpacked(2 * SWEEPS, 1, t)):
            res[where] = res[where] + lat[where] * jnp.where(red[None], outer, 0.0)
    edge_out[0] = res[top]
    edge_out[1] = res[0]

    @pl.when(vert < depth - 1)
    def _():
        edge_copy(0).start()

    @pl.when(vert > 0)
    def _():
        edge_copy(1).start()

    def restrict(m, carry):
        coarse[m] = (
            res[2 * m - 1] + 3.0 * res[2 * m] + 3.0 * res[2 * m + 1] + res[2 * m + 2]
        ) * 0.125
        return carry

    last = levels // 2 - 1
    lax.fori_loop(1, last, restrict, 0, unroll=True)

    @pl.when(vert > 0)
    def _():
        edge_copy(0).wait_recv()

    @pl.when(vert < depth - 1)
    def _():
        edge_copy(1).wait_recv()

    coarse[0] = (edge_in[0] + 3.0 * res[0] + 3.0 * res[1] + res[2]) * 0.125
    coarse[last] = (res[top - 2] + 3.0 * res[top - 1] + 3.0 * res[top] + edge_in[1]) * 0.125

    @pl.when(vert < depth - 1)
    def _():
        low_copy().wait_send()
        edge_copy(0).wait_send()

    @pl.when(vert > 0)
    def _():
        edge_copy(1).wait_send()

    for event in range(2 * SWEEPS):
        for peer in peers:
            end_copy(event, end_buffer(event), vert, peer).wait_send()
    for event in range(2 * SWEEPS + 1):
        @pl.when(ha < width - 1)
        def _():
            halo_copy(event, 0).wait_send()

        @pl.when(ha > 0)
        def _():
            halo_copy(event, 1).wait_send()


def to_tiles(a):
    levels, rows, cols = a.shape
    return a.reshape(levels, rows, cols // LANES, LANES).transpose(0, 2, 1, 3).reshape(
        levels, rows * (cols // LANES), LANES
    )


def from_tiles(a, rows, cols):
    levels = a.shape[0]
    return a.reshape(levels, cols // LANES, rows, LANES).transpose(0, 2, 1, 3).reshape(
        levels, rows, cols
    )


def local(depth, width, rhs, guess, vertical_coupling, lateral_coupling):
    levels, rows, cols = guess.shape
    f32 = jnp.float32
    tile = (8, LANES)
    field = pltpu.VMEM((levels,) + tile, f32)
    events = 2 * SWEEPS + 1
    dma = pltpu.SemaphoreType.DMA
    vmem = pl.BlockSpec(memory_space=pltpu.VMEM)
    smoothed, coarse = pl.pallas_call(
        functools.partial(kernel, depth, width),
        out_shape=(
            jax.ShapeDtypeStruct((levels,) + tile, f32),
            jax.ShapeDtypeStruct((levels // 2,) + tile, f32),
        ),
        in_specs=[vmem] * 4,
        out_specs=(vmem, vmem),
        scratch_shapes=[field] * 8 + [
            pltpu.VMEM(tile, f32),
            pltpu.VMEM((events, 2, levels // 8) + tile, f32),
            pltpu.VMEM((events, 2, levels // 8) + tile, f32),
            pltpu.VMEM((depth, 6) + tile, f32),
            pltpu.VMEM((events - 2, depth, 2) + tile, f32),
            pltpu.VMEM((2, 2 * depth) + tile, f32),
            pltpu.VMEM((2,) + tile, f32),
            pltpu.VMEM((2,) + tile, f32),
            dma, dma,
            dma((events, 2)), dma((events, 2)),
            dma((events - 1, depth)), dma((events - 1, depth)),
            dma((2,)), dma((2,)),
        ],
        compiler_params=pltpu.CompilerParams(
            collective_id=0, has_side_effects=True, vmem_limit_bytes=32 * 1024 * 1024
        ),
        cost_estimate=pl.CostEstimate(
            flops=200 * levels * rows * cols, bytes_accessed=22 * levels * rows * cols,
            transcendentals=0,
        ),
    )(*[to_tiles(a) for a in (rhs, guess, vertical_coupling, lateral_coupling)])
    return from_tiles(smoothed, rows, cols), from_tiles(coarse, rows, cols)


def solution(mesh):
    spec = P("vert", "ha", None)
    return jax.shard_map(
        functools.partial(local, mesh.shape["vert"], mesh.shape["ha"]),
        mesh=mesh,
        in_specs=(spec,) * 4,
        out_specs=(spec, spec),
        check_vma=False,
    )
```

```python
import functools

import jax
import jax.numpy as jnp
from jax import lax
from jax.experimental import pallas as pl
from jax.experimental.pallas import tpu as pltpu
from jax.sharding import PartitionSpec as P

SWEEPS = 2
MESH = pl.DeviceIdType.MESH
LANES = 128


def kernel(
    depth, width, rhs_hbm, guess_hbm, up_hbm, lat_hbm, out, coarse,
    rhs, guess, up, lat,
    inv, fwd, bwd, first_g, last_g, src, work, res,
    low_in, pack, halo, ends0, ends, coef, edge_out, edge_in,
    row0_out, row0_in, row_out, row_in, row_coef, unit_pack, unit_halo, joined,
    low_send, low_recv, halo_send, halo_recv, end_send, end_recv, edge_send, edge_recv,
    load_sem, row_send, row_recv, unit_send, unit_recv,
):
    levels = rhs_hbm.shape[0]
    rows = 4
    half = levels // 2
    chunk = levels // 8
    ha, vert = lax.axis_index("ha"), lax.axis_index("vert")
    sub = lax.broadcasted_iota(jnp.int32, (8, LANES), 0)
    lane = lax.broadcasted_iota(jnp.int32, (8, LANES), 1)
    row = sub % rows
    red = (row + lane) % 2 == 0
    zero = jnp.zeros((8, LANES), jnp.float32)

    def roll(a, by, axis):
        by = by % a.shape[axis]
        return a if by == 0 else pltpu.roll(a, by, axis)

    loads = [
        pltpu.make_async_copy(source, target, load_sem.at[i])
        for i, (source, target) in enumerate(
            ((guess_hbm, guess), (up_hbm, up), (lat_hbm, lat), (rhs_hbm, rhs))
        )
    ]
    for load in loads:
        load.start()

    peers = [lax.rem(vert + o, depth) for o in range(1, depth)]
    barrier = pltpu.get_barrier_semaphore()
    for peer in peers:
        pl.semaphore_signal(barrier, inc=1, device_id=(ha, peer), device_id_type=MESH)

    everyone = [lax.rem(vert + o, depth) for o in range(depth)]

    @pl.when(ha > 0)
    def _():
        for peer in everyone:
            pl.semaphore_signal(barrier, inc=1, device_id=(ha - 1, peer), device_id_type=MESH)

    @pl.when(ha < width - 1)
    def _():
        for peer in everyone:
            pl.semaphore_signal(barrier, inc=1, device_id=(ha + 1, peer), device_id_type=MESH)

    def packed(acc, low_part, high_part, t, colour):
        result = []
        for side, from_row in ((0, rows - 1), (1, 0)):
            odd = (from_row + colour) % 2
            both = jnp.where(
                (lane % 2 == odd)[None], low_part, roll(high_part, -1 if odd else 1, 2)
            )
            both = roll(both, t - from_row, 1)
            result.append(both if acc is None else jnp.where((row == t)[None], both, acc[side]))
        return result

    def halo_copy(event, side):
        target = ha + 1 if side == 0 else ha - 1
        return pltpu.make_async_remote_copy(
            src_ref=pack.at[event, side], dst_ref=halo.at[event, side],
            send_sem=halo_send.at[event, side], recv_sem=halo_recv.at[event, side],
            device_id=(target, vert), device_id_type=MESH,
        )

    def halo_start(event, acc):
        pack[event, 0] = acc[0]
        pack[event, 1] = acc[1]

        @pl.when(ha < width - 1)
        def _():
            halo_copy(event, 0).start()

        @pl.when(ha > 0)
        def _():
            halo_copy(event, 1).start()

    def halo_wait(event):
        @pl.when(ha > 0)
        def _():
            halo_copy(event, 0).wait_recv()

        @pl.when(ha < width - 1)
        def _():
            halo_copy(event, 1).wait_recv()

    def unpacked(planes, colour, t):
        lows, highs = [], []
        for side, from_row, to_row in ((0, rows - 1, 0), (1, 0, rows - 1)):
            odd = (from_row + colour) % 2
            both = roll(planes[side], to_row - t, 1)
            lows.append(both)
            highs.append(roll(both, 1 if odd else -1, 2))
        below, above = (row == 0)[None], (row == rows - 1)[None]
        return [
            jnp.where(below, pair[0], jnp.where(above, pair[1], 0.0)) for pair in (lows, highs)
        ]

    def lateral_inner(v):
        left = roll(v, 1, 2)
        right = roll(v, -1, 2)
        left = jnp.where(
            (lane == 0)[None], jnp.where((sub < rows)[None], 0.0, roll(left, rows, 1)), left
        )
        right = jnp.where(
            (lane == LANES - 1)[None], jnp.where((sub < rows)[None], roll(right, rows, 1), 0.0),
            right,
        )
        below = jnp.where((row == 0)[None], 0.0, roll(v, 1, 1))
        above = jnp.where((row == rows - 1)[None], 0.0, roll(v, -1, 1))
        return left + right + below + above

    def part(t):
        return pl.ds(t * chunk, chunk)

    def end_copy(event, buffer, slot, peer):
        return pltpu.make_async_remote_copy(
            src_ref=buffer.at[slot], dst_ref=buffer.at[slot],
            send_sem=end_send.at[event, peer], recv_sem=end_recv.at[event, slot],
            device_id=(ha, peer), device_id_type=MESH,
        )

    def end_buffer(event):
        return ends0 if event == 0 else ends.at[event - 1]

    def row_buffers(event):
        return (row0_out, row0_in) if event == 0 else (row_out.at[event - 1], row_in.at[event - 1])

    def row_copy(event, side, slot, peer):
        source, target = row_buffers(event)
        return pltpu.make_async_remote_copy(
            src_ref=source.at[side], dst_ref=target.at[side, slot],
            send_sem=row_send.at[event, side, peer], recv_sem=row_recv.at[event, side, slot],
            device_id=(ha + 1 if side == 0 else ha - 1, peer), device_id_type=MESH,
        )

    def unit_copy(colour, side):
        return pltpu.make_async_remote_copy(
            src_ref=unit_pack.at[colour, side], dst_ref=unit_halo.at[colour, side],
            send_sem=unit_send.at[colour, side], recv_sem=unit_recv.at[colour, side],
            device_id=(ha + 1 if side == 0 else ha - 1, vert), device_id_type=MESH,
        )

    def to_sides(act):
        @pl.when(ha < width - 1)
        def _():
            act(0)

        @pl.when(ha > 0)
        def _():
            act(1)

    def from_sides(act):
        @pl.when(ha > 0)
        def _():
            act(0)

        @pl.when(ha < width - 1)
        def _():
            act(1)

    def rows_start(event, items):
        source, _ = row_buffers(event)
        for side, from_row in ((0, rows - 1), (1, 0)):
            for first in range(0, len(items), rows):
                tile = zero
                for t, item in enumerate(items[first:first + rows]):
                    tile = jnp.where(row == t, roll(item, t - from_row, 0), tile)
                source[side, first // rows] = tile

        def start(side):
            for peer in everyone:
                row_copy(event, side, vert, peer).start()

        to_sides(start)

    def rows_wait(event):
        def wait(side):
            for peer in everyone:
                row_copy(event, side, peer, peer).wait_recv()

        from_sides(wait)

    def row_item(event, slot, item):
        _, target = row_buffers(event)
        t = item % rows
        return jnp.where(
            row == 0, roll(target[0, slot, item // rows], -t, 0),
            jnp.where(row == rows - 1, roll(target[1, slot, item // rows], rows - 1 - t, 0), 0.0),
        )

    def units_start(colour):
        for i, field in enumerate((first_g, last_g)):
            acc = None
            for t in range(4):
                acc = packed(acc, field[part(t)], field[part(t + 4)], t, colour)
            unit_pack[colour, 0, i] = acc[0]
            unit_pack[colour, 1, i] = acc[1]
        to_sides(lambda side: unit_copy(colour, side).start())

    def spread(value, side, colour):
        sign = 1 if side == 0 else -1
        kept = jnp.where(row == (0 if side == 0 else rows - 1), value, 0.0)
        total = kept
        for by in range(1, rows):
            total = total + roll(kept, sign * by, 0)
        odd = ((rows - 1 if side == 0 else 0) + colour) % 2
        return jnp.where(lane % 2 == odd, total, roll(total, -1 if odd else 1, 1))

    def join_planes(event, colour, from_b, from_a):
        for side in range(2):
            b = spread(from_b, side, colour)
            a = spread(from_a, side, colour)
            joined[side] = (
                halo[event, side] + unit_halo[colour, side, 0] * b + unit_halo[colour, side, 1] * a
            )

    def low_copy():
        return pltpu.make_async_remote_copy(
            src_ref=up.at[levels - 1], dst_ref=low_in, send_sem=low_send, recv_sem=low_recv,
            device_id=(ha, vert + 1), device_id_type=MESH,
        )

    def edge_copy(side):
        target = vert + 1 if side == 0 else vert - 1
        return pltpu.make_async_remote_copy(
            src_ref=edge_out.at[side], dst_ref=edge_in.at[side],
            send_sem=edge_send.at[side], recv_sem=edge_recv.at[side],
            device_id=(ha, target), device_id_type=MESH,
        )

    @pl.when(ha == 0)
    def _():
        for event in range(2 * SWEEPS + 1):
            halo[event, 0] = jnp.zeros(halo.shape[2:], jnp.float32)
        for colour in range(2):
            unit_halo[colour, 0] = jnp.zeros(unit_halo.shape[2:], jnp.float32)
        row0_in[0] = jnp.zeros(row0_in.shape[1:], jnp.float32)
        for event in range(2 * SWEEPS - 1):
            row_in[event, 0] = jnp.zeros(row_in.shape[2:], jnp.float32)

    @pl.when(ha == width - 1)
    def _():
        for event in range(2 * SWEEPS + 1):
            halo[event, 1] = jnp.zeros(halo.shape[2:], jnp.float32)
        for colour in range(2):
            unit_halo[colour, 1] = jnp.zeros(unit_halo.shape[2:], jnp.float32)
        row0_in[1] = jnp.zeros(row0_in.shape[1:], jnp.float32)
        for event in range(2 * SWEEPS - 1):
            row_in[event, 1] = jnp.zeros(row_in.shape[2:], jnp.float32)

    @pl.when(vert == 0)
    def _():
        low_in[...] = zero
        edge_in[0] = zero

    @pl.when(vert == depth - 1)
    def _():
        edge_in[1] = zero

    loads[0].wait()
    acc = None
    for t in range(4):
        acc = packed(acc, guess[part(t)], guess[part(t + 4)], t, 1)

    greeted = (ha > 0).astype(jnp.int32) + (ha < width - 1).astype(jnp.int32)
    pl.semaphore_wait(barrier, depth - 1 + depth * greeted)

    loads[1].wait()

    @pl.when(vert < depth - 1)
    def _():
        low_copy().start()

    halo_start(0, acc)
    loads[2].wait()
    loads[3].wait()

    def partial_source(field):
        def body(t, carry):
            at = pl.ds(pl.multiple_of(t * chunk, chunk), chunk)
            src[at] = rhs[at] + lat[at] * lateral_inner(field[at])
            return carry
        lax.fori_loop(0, 8, body, 0, unroll=True)

    partial_source(guess)

    @pl.when(vert > 0)
    def _():
        low_copy().wait_recv()

    low0 = low_in[...]
    top = levels - 1
    up_top = up[top]

    def eliminate(k, carry, start):
        piv_l, g_l, piv_u, g_u = carry
        j = top - k
        low_k = low0 if start else up[k - 1]
        up_k = up[k]
        inv_k = 1.0 / (4.0 * lat[k] + up_k + low_k - low_k * piv_l)
        piv_l = up_k * inv_k
        g_l = inv_k if start else low_k * inv_k * g_l
        inv[k] = inv_k
        fwd[k] = low_k * inv_k
        bwd[k] = piv_l
        first_g[k] = g_l
        low_j, up_j = up[j - 1], up[j]
        inv_j = 1.0 / (4.0 * lat[j] + up_j + low_j - up_j * piv_u)
        piv_u = low_j * inv_j
        g_u = inv_j if start else up_j * inv_j * g_u
        inv[j] = inv_j
        fwd[j] = up_j * inv_j
        bwd[j] = piv_u
        last_g[j] = g_u
        return piv_l, g_l, piv_u, g_u

    carry = eliminate(0, (zero, zero, zero, zero), True)
    carry = lax.fori_loop(1, half, lambda k, c: eliminate(k, c, False), carry, unroll=True)
    piv_l, g_l, piv_u, g_u = carry
    meet = 1.0 / (1.0 - piv_l * piv_u)
    fa = g_l * meet
    fb = piv_u * fa
    lb = g_u * meet
    la = piv_l * lb
    first_g[half - 1] = fa
    first_g[half] = fb
    last_g[half] = lb
    last_g[half - 1] = la

    def respond(i, carry):
        fa, la, fb, lb = carry
        k = half - 1 - i
        j = half + i
        bk, bj = bwd[k], bwd[j]
        fa = first_g[k] + bk * fa
        la = bk * la
        fb = bj * fb
        lb = last_g[j] + bj * lb
        first_g[k] = fa
        last_g[k] = la
        first_g[j] = fb
        last_g[j] = lb
        return fa, la, fb, lb

    fa, la, fb, lb = lax.fori_loop(1, half, respond, (fa, la, fb, lb), unroll=True)
    own = [low0 * fa, low0 * fb, up_top * la, up_top * lb]

    def interface_coefficients(table, own, low0, up_top, coef):
        slope_b, slope_a = zero, zero
        below = [zero] * (2 * depth)
        above = [zero] * (2 * depth)
        for e in range(depth - 1):
            v_f, v_l, w_f, w_l = table[e]
            keep = (e < vert).astype(jnp.float32)
            ratio = v_l * slope_b / (1.0 - v_f * slope_b)
            gain = keep * (v_l + ratio * v_f) + (1.0 - keep)
            below = [gain * b if n < 2 * e else b for n, b in enumerate(below)]
            below[2 * e] = keep * ratio
            below[2 * e + 1] = jnp.full((8, LANES), keep)
            slope_b = keep * (w_l + ratio * w_f) + (1.0 - keep) * slope_b
        for e in range(depth - 1, 0, -1):
            v_f, v_l, w_f, w_l = table[e]
            keep = (e > vert).astype(jnp.float32)
            ratio = w_f * slope_a / (1.0 - w_l * slope_a)
            gain = keep * (w_f + ratio * w_l) + (1.0 - keep)
            above = [gain * a if n > 2 * e + 1 else a for n, a in enumerate(above)]
            above[2 * e] = jnp.full((8, LANES), keep)
            above[2 * e + 1] = keep * ratio
            slope_a = keep * (v_f + ratio * v_l) + (1.0 - keep) * slope_a
        v_f, v_l, w_f, w_l = own
        c_ss, c_tt = 1.0 - slope_b * v_f, 1.0 - slope_a * w_l
        c_st, c_ts = slope_b * w_f, slope_a * v_l
        scale = 1.0 / (c_ss * c_tt - c_st * c_ts)
        for n in range(2 * depth):
            mine = (vert == n // 2).astype(jnp.float32)
            r_b = below[n] + mine * slope_b if n % 2 == 0 else below[n]
            r_a = above[n] + mine * slope_a if n % 2 == 1 else above[n]
            coef[0, n] = low0 * scale * (r_b * c_tt + c_st * r_a)
            coef[1, n] = up_top * scale * (c_ss * r_a + c_ts * r_b)

    reach = {}
    planes = halo.at[0]
    for event in range(2 * SWEEPS):
        colour = event % 2
        chosen = red if colour == 0 else jnp.logical_not(red)
        if event == 0:
            halo_wait(0)
        dot_f, dot_l = zero, zero
        for t in range(4):
            for where, outer in zip((part(t), part(t + 4)), unpacked(planes, 1 - colour, t)):
                full = src[where] + lat[where] * outer
                src[where] = full
                dot_f = dot_f + jnp.sum(full * first_g[where], axis=0)
                dot_l = dot_l + jnp.sum(full * last_g[where], axis=0)
        buffer = end_buffer(event)
        buffer[vert, 0] = dot_f
        buffer[vert, 1] = dot_l
        if event == 0:
            for i in range(4):
                buffer[vert, 2 + i] = own[i]
        rows_start(event, [dot_f, dot_l] + (own + [low0, up_top] if event == 0 else []))
        for peer in peers:
            end_copy(event, buffer, vert, peer).start()
        if event == 0:
            units_start(0)

        def forward(k, carry):
            f_l, f_u = carry
            j = top - k
            f_l = src[k] * inv[k] + fwd[k] * f_l
            f_u = src[j] * inv[j] + fwd[j] * f_u
            work[k] = f_l
            work[j] = f_u
            return f_l, f_u

        f_l, f_u = lax.fori_loop(0, half, forward, (zero, zero), unroll=True)
        y_l = (f_l + piv_l * f_u) * meet
        y_u = f_u + piv_u * y_l
        work[half - 1] = y_l
        work[half] = y_u

        def backward(i, carry):
            y_l, y_u = carry
            k = half - 1 - i
            j = half + i
            y_l = work[k] + bwd[k] * y_l
            y_u = work[j] + bwd[j] * y_u
            work[k] = y_l
            work[j] = y_u
            return y_l, y_u

        lax.fori_loop(1, half, backward, (y_l, y_u), unroll=True)
        acc = None
        for t in range(4):
            acc = packed(acc, work[part(t)], work[part(t + 4)], t, colour)
        halo_start(event + 1, acc)
        if event == 0:
            units_start(1)
        for peer in peers:
            end_copy(event, buffer, peer, peer).wait_recv()
        if event == 0:
            table = [[ends0[e, 2 + i] for i in range(4)] for e in range(depth)]
            interface_coefficients(table, own, low0, up_top, coef)
        from_b, from_a = zero, zero
        for n in range(2 * depth):
            value = buffer[n // 2, n % 2]
            from_b = from_b + coef[0, n] * value
            from_a = from_a + coef[1, n] * value
        reach[colour] = (from_b, from_a)
        old = guess if event == 0 else out
        for t in range(8):
            where = part(t)
            new = work[where] + first_g[where] * from_b + last_g[where] * from_a
            out[where] = jnp.where(chosen[None], new, old[where])
        if event == 2 * SWEEPS - 1:
            def keep_source(t, carry):
                at = pl.ds(pl.multiple_of(t * chunk, chunk), chunk)
                inner = rhs[at] + lat[at] * lateral_inner(out[at])
                src[at] = jnp.where(red[None], inner, src[at])
                return carry
            lax.fori_loop(0, 8, keep_source, 0, unroll=True)
        else:
            partial_source(out)
        rows_wait(event)
        if event == 0:
            table = [[row_item(0, e, 2 + i) for i in range(4)] for e in range(depth)]
            mine = [row_item(0, vert, 2 + i) for i in range(6)]
            interface_coefficients(table, mine[:4], mine[4], mine[5], row_coef)
        from_b, from_a = zero, zero
        for n in range(2 * depth):
            value = row_item(event, n // 2, n % 2)
            from_b = from_b + row_coef[0, n] * value
            from_a = from_a + row_coef[1, n] * value
        if event < 2:
            from_sides(lambda side: unit_copy(colour, side).wait_recv())
        halo_wait(event + 1)
        join_planes(event + 1, colour, from_b, from_a)
        planes = joined

    from_b = jnp.where(red, reach[0][0], reach[1][0])
    from_a = jnp.where(red, reach[0][1], reach[1][1])

    def applied(k):
        low_k = low0 if k == 0 else up[k - 1]
        under = from_b if k == 0 else low_k * out[k - 1]
        over = from_a if k == top else up[k] * out[k + 1]
        return (4.0 * lat[k] + up[k] + low_k) * out[k] - over - under

    for t in range(4):
        for where, outer in zip((part(t), part(t + 4)), unpacked(joined, 1, t)):
            src[where] = src[where] + lat[where] * jnp.where(red[None], outer, 0.0)
    bottom_res = src[0] - applied(0)
    top_res = src[top] - applied(top)
    res[0] = bottom_res
    res[top] = top_res
    edge_out[0] = top_res
    edge_out[1] = bottom_res

    @pl.when(vert < depth - 1)
    def _():
        edge_copy(0).start()

    @pl.when(vert > 0)
    def _():
        edge_copy(1).start()

    def inner_level(k, carry):
        low_k, up_k = up[k - 1], up[k]
        res[k] = src[k] - (
            (4.0 * lat[k] + up_k + low_k) * out[k] - up_k * out[k + 1] - low_k * out[k - 1]
        )
        return carry

    lax.fori_loop(1, top, inner_level, 0, unroll=True)

    def restrict(m, carry):
        coarse[m] = (
            res[2 * m - 1] + 3.0 * res[2 * m] + 3.0 * res[2 * m + 1] + res[2 * m + 2]
        ) * 0.125
        return carry

    last = levels // 2 - 1
    lax.fori_loop(1, last, restrict, 0, unroll=True)

    @pl.when(vert > 0)
    def _():
        edge_copy(0).wait_recv()

    @pl.when(vert < depth - 1)
    def _():
        edge_copy(1).wait_recv()

    coarse[0] = (edge_in[0] + 3.0 * res[0] + 3.0 * res[1] + res[2]) * 0.125
    coarse[last] = (res[top - 2] + 3.0 * res[top - 1] + 3.0 * res[top] + edge_in[1]) * 0.125

    @pl.when(vert < depth - 1)
    def _():
        low_copy().wait_send()
        edge_copy(0).wait_send()

    @pl.when(vert > 0)
    def _():
        edge_copy(1).wait_send()

    for event in range(2 * SWEEPS):
        for peer in peers:
            end_copy(event, end_buffer(event), vert, peer).wait_send()

        def sent(side):
            for peer in everyone:
                row_copy(event, side, vert, peer).wait_send()

        to_sides(sent)
    for colour in range(2):
        to_sides(lambda side: unit_copy(colour, side).wait_send())
    for event in range(2 * SWEEPS + 1):
        @pl.when(ha < width - 1)
        def _():
            halo_copy(event, 0).wait_send()

        @pl.when(ha > 0)
        def _():
            halo_copy(event, 1).wait_send()


def to_tiles(a):
    levels, rows, cols = a.shape
    return a.reshape(levels, rows, cols // LANES, LANES).transpose(0, 2, 1, 3).reshape(
        levels, rows * (cols // LANES), LANES
    )


def from_tiles(a, rows, cols):
    levels = a.shape[0]
    return a.reshape(levels, cols // LANES, rows, LANES).transpose(0, 2, 1, 3).reshape(
        levels, rows, cols
    )


def local(depth, width, rhs, guess, vertical_coupling, lateral_coupling):
    levels, rows, cols = guess.shape
    f32 = jnp.float32
    tile = (8, LANES)
    field = pltpu.VMEM((levels,) + tile, f32)
    events = 2 * SWEEPS + 1
    dma = pltpu.SemaphoreType.DMA
    vmem = pl.BlockSpec(memory_space=pltpu.VMEM)
    smoothed, coarse = pl.pallas_call(
        functools.partial(kernel, depth, width),
        out_shape=(
            jax.ShapeDtypeStruct((levels,) + tile, f32),
            jax.ShapeDtypeStruct((levels // 2,) + tile, f32),
        ),
        in_specs=[pl.BlockSpec(memory_space=pl.ANY)] * 4,
        out_specs=(vmem, vmem),
        scratch_shapes=[field] * 12 + [
            pltpu.VMEM(tile, f32),
            pltpu.VMEM((events, 2, levels // 8) + tile, f32),
            pltpu.VMEM((events, 2, levels // 8) + tile, f32),
            pltpu.VMEM((depth, 6) + tile, f32),
            pltpu.VMEM((events - 2, depth, 2) + tile, f32),
            pltpu.VMEM((2, 2 * depth) + tile, f32),
            pltpu.VMEM((2,) + tile, f32),
            pltpu.VMEM((2,) + tile, f32),
            pltpu.VMEM((2, 2) + tile, f32),
            pltpu.VMEM((2, depth, 2) + tile, f32),
            pltpu.VMEM((events - 2, 2, 1) + tile, f32),
            pltpu.VMEM((events - 2, 2, depth, 1) + tile, f32),
            pltpu.VMEM((2, 2 * depth) + tile, f32),
            pltpu.VMEM((2, 2, 2, levels // 8) + tile, f32),
            pltpu.VMEM((2, 2, 2, levels // 8) + tile, f32),
            pltpu.VMEM((2, levels // 8) + tile, f32),
            dma, dma,
            dma((events, 2)), dma((events, 2)),
            dma((events - 1, depth)), dma((events - 1, depth)),
            dma((2,)), dma((2,)), dma((4,)),
            dma((events - 1, 2, depth)), dma((events - 1, 2, depth)), dma((2, 2)), dma((2, 2)),
        ],
        compiler_params=pltpu.CompilerParams(
            collective_id=0, has_side_effects=True, vmem_limit_bytes=56 * 1024 * 1024
        ),
        cost_estimate=pl.CostEstimate(
            flops=200 * levels * rows * cols, bytes_accessed=22 * levels * rows * cols,
            transcendentals=0,
        ),
    )(*[to_tiles(a) for a in (rhs, guess, vertical_coupling, lateral_coupling)])
    return from_tiles(smoothed, rows, cols), from_tiles(coarse, rows, cols)


def solution(mesh):
    spec = P("vert", "ha", None)
    return jax.shard_map(
        functools.partial(local, mesh.shape["vert"], mesh.shape["ha"]),
        mesh=mesh,
        in_specs=(spec,) * 4,
        out_specs=(spec, spec),
        check_vma=False,
    )
```

```python
import functools

import jax
import jax.numpy as jnp
from jax import lax
from jax.experimental import pallas as pl
from jax.experimental.pallas import tpu as pltpu
from jax.sharding import PartitionSpec as P

SWEEPS = 2
MESH = pl.DeviceIdType.MESH
LANES = 128


def kernel(
    depth, width, rhs_hbm, guess_hbm, up_hbm, lat_hbm, out_hbm, coarse_hbm,
    out, coarse, rhs, guess, up, lat,
    inv, fwd, bwd, first_g, last_g, src, work, res,
    low_in, pack, halo, ends0, ends, coef, edge_out, edge_in,
    row0_out, row0_in, row_out, row_in, row_coef, unit_pack, unit_halo, joined,
    low_send, low_recv, halo_send, halo_recv, end_send, end_recv, edge_send, edge_recv,
    load_sem, store_sem, row_send, row_recv, unit_send, unit_recv,
):
    levels = rhs_hbm.shape[0]
    rows = 4
    half = levels // 2
    chunk = levels // 8
    ha, vert = lax.axis_index("ha"), lax.axis_index("vert")
    sub = lax.broadcasted_iota(jnp.int32, (8, LANES), 0)
    lane = lax.broadcasted_iota(jnp.int32, (8, LANES), 1)
    row = sub % rows
    red = (row + lane) % 2 == 0
    zero = jnp.zeros((8, LANES), jnp.float32)

    def roll(a, by, axis):
        by = by % a.shape[axis]
        return a if by == 0 else pltpu.roll(a, by, axis)

    loads = [
        pltpu.make_async_copy(source, target, load_sem.at[i])
        for i, (source, target) in enumerate(
            ((guess_hbm, guess), (up_hbm, up), (lat_hbm, lat), (rhs_hbm, rhs))
        )
    ]
    for load in loads:
        load.start()

    peers = [lax.rem(vert + o, depth) for o in range(1, depth)]
    barrier = pltpu.get_barrier_semaphore()
    for peer in peers:
        pl.semaphore_signal(barrier, inc=1, device_id=(ha, peer), device_id_type=MESH)

    everyone = [lax.rem(vert + o, depth) for o in range(depth)]

    @pl.when(ha > 0)
    def _():
        for peer in everyone:
            pl.semaphore_signal(barrier, inc=1, device_id=(ha - 1, peer), device_id_type=MESH)

    @pl.when(ha < width - 1)
    def _():
        for peer in everyone:
            pl.semaphore_signal(barrier, inc=1, device_id=(ha + 1, peer), device_id_type=MESH)

    def packed(acc, low_part, high_part, t, colour):
        result = []
        for side, from_row in ((0, rows - 1), (1, 0)):
            odd = (from_row + colour) % 2
            both = jnp.where(
                (lane % 2 == odd)[None], low_part, roll(high_part, -1 if odd else 1, 2)
            )
            both = roll(both, t - from_row, 1)
            result.append(both if acc is None else jnp.where((row == t)[None], both, acc[side]))
        return result

    def halo_copy(event, side):
        target = ha + 1 if side == 0 else ha - 1
        return pltpu.make_async_remote_copy(
            src_ref=pack.at[event, side], dst_ref=halo.at[event, side],
            send_sem=halo_send.at[event, side], recv_sem=halo_recv.at[event, side],
            device_id=(target, vert), device_id_type=MESH,
        )

    def halo_start(event, acc):
        pack[event, 0] = acc[0]
        pack[event, 1] = acc[1]

        @pl.when(ha < width - 1)
        def _():
            halo_copy(event, 0).start()

        @pl.when(ha > 0)
        def _():
            halo_copy(event, 1).start()

    def halo_wait(event):
        @pl.when(ha > 0)
        def _():
            halo_copy(event, 0).wait_recv()

        @pl.when(ha < width - 1)
        def _():
            halo_copy(event, 1).wait_recv()

    def unpacked(planes, colour, t):
        lows, highs = [], []
        for side, from_row, to_row in ((0, rows - 1, 0), (1, 0, rows - 1)):
            odd = (from_row + colour) % 2
            both = roll(planes[side], to_row - t, 1)
            lows.append(both)
            highs.append(roll(both, 1 if odd else -1, 2))
        below, above = (row == 0)[None], (row == rows - 1)[None]
        return [
            jnp.where(below, pair[0], jnp.where(above, pair[1], 0.0)) for pair in (lows, highs)
        ]

    def lateral_inner(v):
        left = roll(v, 1, 2)
        right = roll(v, -1, 2)
        left = jnp.where(
            (lane == 0)[None], jnp.where((sub < rows)[None], 0.0, roll(left, rows, 1)), left
        )
        right = jnp.where(
            (lane == LANES - 1)[None], jnp.where((sub < rows)[None], roll(right, rows, 1), 0.0),
            right,
        )
        below = jnp.where((row == 0)[None], 0.0, roll(v, 1, 1))
        above = jnp.where((row == rows - 1)[None], 0.0, roll(v, -1, 1))
        return left + right + below + above

    def part(t):
        return pl.ds(t * chunk, chunk)

    def end_copy(event, buffer, slot, peer):
        return pltpu.make_async_remote_copy(
            src_ref=buffer.at[slot], dst_ref=buffer.at[slot],
            send_sem=end_send.at[event, peer], recv_sem=end_recv.at[event, slot],
            device_id=(ha, peer), device_id_type=MESH,
        )

    def end_buffer(event):
        return ends0 if event == 0 else ends.at[event - 1]

    def row_buffers(event):
        return (row0_out, row0_in) if event == 0 else (row_out.at[event - 1], row_in.at[event - 1])

    def row_copy(event, side, slot, peer):
        source, target = row_buffers(event)
        return pltpu.make_async_remote_copy(
            src_ref=source.at[side], dst_ref=target.at[side, slot],
            send_sem=row_send.at[event, side, peer], recv_sem=row_recv.at[event, side, slot],
            device_id=(ha + 1 if side == 0 else ha - 1, peer), device_id_type=MESH,
        )

    def unit_copy(colour, side):
        return pltpu.make_async_remote_copy(
            src_ref=unit_pack.at[colour, side], dst_ref=unit_halo.at[colour, side],
            send_sem=unit_send.at[colour, side], recv_sem=unit_recv.at[colour, side],
            device_id=(ha + 1 if side == 0 else ha - 1, vert), device_id_type=MESH,
        )

    def to_sides(act):
        @pl.when(ha < width - 1)
        def _():
            act(0)

        @pl.when(ha > 0)
        def _():
            act(1)

    def from_sides(act):
        @pl.when(ha > 0)
        def _():
            act(0)

        @pl.when(ha < width - 1)
        def _():
            act(1)

    def rows_start(event, items):
        source, _ = row_buffers(event)
        for side, from_row in ((0, rows - 1), (1, 0)):
            for first in range(0, len(items), rows):
                tile = zero
                for t, item in enumerate(items[first:first + rows]):
                    tile = jnp.where(row == t, roll(item, t - from_row, 0), tile)
                source[side, first // rows] = tile

        def start(side):
            for peer in everyone:
                row_copy(event, side, vert, peer).start()

        to_sides(start)

    def rows_wait(event):
        def wait(side):
            for peer in everyone:
                row_copy(event, side, peer, peer).wait_recv()

        from_sides(wait)

    def row_item(event, slot, item):
        _, target = row_buffers(event)
        t = item % rows
        return jnp.where(
            row == 0, roll(target[0, slot, item // rows], -t, 0),
            jnp.where(row == rows - 1, roll(target[1, slot, item // rows], rows - 1 - t, 0), 0.0),
        )

    def units_start(colour):
        for i, field in enumerate((first_g, last_g)):
            acc = None
            for t in range(4):
                acc = packed(acc, field[part(t)], field[part(t + 4)], t, colour)
            unit_pack[colour, 0, i] = acc[0]
            unit_pack[colour, 1, i] = acc[1]
        to_sides(lambda side: unit_copy(colour, side).start())

    def spread(value, side, colour):
        sign = 1 if side == 0 else -1
        kept = jnp.where(row == (0 if side == 0 else rows - 1), value, 0.0)
        total = kept
        for by in range(1, rows):
            total = total + roll(kept, sign * by, 0)
        odd = ((rows - 1 if side == 0 else 0) + colour) % 2
        return jnp.where(lane % 2 == odd, total, roll(total, -1 if odd else 1, 1))

    def join_planes(event, colour, from_b, from_a):
        for side in range(2):
            b = spread(from_b, side, colour)
            a = spread(from_a, side, colour)
            joined[side] = (
                halo[event, side] + unit_halo[colour, side, 0] * b + unit_halo[colour, side, 1] * a
            )

    def low_copy():
        return pltpu.make_async_remote_copy(
            src_ref=up.at[levels - 1], dst_ref=low_in, send_sem=low_send, recv_sem=low_recv,
            device_id=(ha, vert + 1), device_id_type=MESH,
        )

    def edge_copy(side):
        target = vert + 1 if side == 0 else vert - 1
        return pltpu.make_async_remote_copy(
            src_ref=edge_out.at[side], dst_ref=edge_in.at[side],
            send_sem=edge_send.at[side], recv_sem=edge_recv.at[side],
            device_id=(ha, target), device_id_type=MESH,
        )

    @pl.when(ha == 0)
    def _():
        for event in range(2 * SWEEPS + 1):
            halo[event, 0] = jnp.zeros(halo.shape[2:], jnp.float32)
        for colour in range(2):
            unit_halo[colour, 0] = jnp.zeros(unit_halo.shape[2:], jnp.float32)
        row0_in[0] = jnp.zeros(row0_in.shape[1:], jnp.float32)
        for event in range(2 * SWEEPS - 1):
            row_in[event, 0] = jnp.zeros(row_in.shape[2:], jnp.float32)

    @pl.when(ha == width - 1)
    def _():
        for event in range(2 * SWEEPS + 1):
            halo[event, 1] = jnp.zeros(halo.shape[2:], jnp.float32)
        for colour in range(2):
            unit_halo[colour, 1] = jnp.zeros(unit_halo.shape[2:], jnp.float32)
        row0_in[1] = jnp.zeros(row0_in.shape[1:], jnp.float32)
        for event in range(2 * SWEEPS - 1):
            row_in[event, 1] = jnp.zeros(row_in.shape[2:], jnp.float32)

    @pl.when(vert == 0)
    def _():
        low_in[...] = zero
        edge_in[0] = zero

    @pl.when(vert == depth - 1)
    def _():
        edge_in[1] = zero

    loads[0].wait()
    acc = None
    for t in range(4):
        acc = packed(acc, guess[part(t)], guess[part(t + 4)], t, 1)

    greeted = (ha > 0).astype(jnp.int32) + (ha < width - 1).astype(jnp.int32)
    pl.semaphore_wait(barrier, depth - 1 + depth * greeted)

    loads[1].wait()

    @pl.when(vert < depth - 1)
    def _():
        low_copy().start()

    halo_start(0, acc)
    loads[2].wait()
    loads[3].wait()

    def partial_source(field):
        def body(t, carry):
            at = pl.ds(pl.multiple_of(t * chunk, chunk), chunk)
            src[at] = rhs[at] + lat[at] * lateral_inner(field[at])
            return carry
        lax.fori_loop(0, 8, body, 0, unroll=True)

    partial_source(guess)

    @pl.when(vert > 0)
    def _():
        low_copy().wait_recv()

    low0 = low_in[...]
    top = levels - 1
    up_top = up[top]

    def eliminate(k, carry, start):
        piv_l, g_l, piv_u, g_u = carry
        j = top - k
        low_k = low0 if start else up[k - 1]
        up_k = up[k]
        inv_k = 1.0 / (4.0 * lat[k] + up_k + low_k - low_k * piv_l)
        piv_l = up_k * inv_k
        g_l = inv_k if start else low_k * inv_k * g_l
        inv[k] = inv_k
        fwd[k] = low_k * inv_k
        bwd[k] = piv_l
        first_g[k] = g_l
        low_j, up_j = up[j - 1], up[j]
        inv_j = 1.0 / (4.0 * lat[j] + up_j + low_j - up_j * piv_u)
        piv_u = low_j * inv_j
        g_u = inv_j if start else up_j * inv_j * g_u
        inv[j] = inv_j
        fwd[j] = up_j * inv_j
        bwd[j] = piv_u
        last_g[j] = g_u
        return piv_l, g_l, piv_u, g_u

    carry = eliminate(0, (zero, zero, zero, zero), True)
    carry = lax.fori_loop(1, half, lambda k, c: eliminate(k, c, False), carry, unroll=True)
    piv_l, g_l, piv_u, g_u = carry
    meet = 1.0 / (1.0 - piv_l * piv_u)
    fa = g_l * meet
    fb = piv_u * fa
    lb = g_u * meet
    la = piv_l * lb
    first_g[half - 1] = fa
    first_g[half] = fb
    last_g[half] = lb
    last_g[half - 1] = la

    def respond(i, carry):
        fa, la, fb, lb = carry
        k = half - 1 - i
        j = half + i
        bk, bj = bwd[k], bwd[j]
        fa = first_g[k] + bk * fa
        la = bk * la
        fb = bj * fb
        lb = last_g[j] + bj * lb
        first_g[k] = fa
        last_g[k] = la
        first_g[j] = fb
        last_g[j] = lb
        return fa, la, fb, lb

    fa, la, fb, lb = lax.fori_loop(1, half, respond, (fa, la, fb, lb), unroll=True)
    own = [low0 * fa, low0 * fb, up_top * la, up_top * lb]

    def interface_coefficients(table, own, low0, up_top, coef):
        slope_b, slope_a = zero, zero
        below = [zero] * (2 * depth)
        above = [zero] * (2 * depth)
        for e in range(depth - 1):
            v_f, v_l, w_f, w_l = table[e]
            keep = (e < vert).astype(jnp.float32)
            ratio = v_l * slope_b / (1.0 - v_f * slope_b)
            gain = keep * (v_l + ratio * v_f) + (1.0 - keep)
            below = [gain * b if n < 2 * e else b for n, b in enumerate(below)]
            below[2 * e] = keep * ratio
            below[2 * e + 1] = jnp.full((8, LANES), keep)
            slope_b = keep * (w_l + ratio * w_f) + (1.0 - keep) * slope_b
        for e in range(depth - 1, 0, -1):
            v_f, v_l, w_f, w_l = table[e]
            keep = (e > vert).astype(jnp.float32)
            ratio = w_f * slope_a / (1.0 - w_l * slope_a)
            gain = keep * (w_f + ratio * w_l) + (1.0 - keep)
            above = [gain * a if n > 2 * e + 1 else a for n, a in enumerate(above)]
            above[2 * e] = jnp.full((8, LANES), keep)
            above[2 * e + 1] = keep * ratio
            slope_a = keep * (v_f + ratio * v_l) + (1.0 - keep) * slope_a
        v_f, v_l, w_f, w_l = own
        c_ss, c_tt = 1.0 - slope_b * v_f, 1.0 - slope_a * w_l
        c_st, c_ts = slope_b * w_f, slope_a * v_l
        scale = 1.0 / (c_ss * c_tt - c_st * c_ts)
        for n in range(2 * depth):
            mine = (vert == n // 2).astype(jnp.float32)
            r_b = below[n] + mine * slope_b if n % 2 == 0 else below[n]
            r_a = above[n] + mine * slope_a if n % 2 == 1 else above[n]
            coef[0, n] = low0 * scale * (r_b * c_tt + c_st * r_a)
            coef[1, n] = up_top * scale * (c_ss * r_a + c_ts * r_b)

    reach = {}
    planes = halo.at[0]
    for event in range(2 * SWEEPS):
        colour = event % 2
        chosen = red if colour == 0 else jnp.logical_not(red)
        if event == 0:
            halo_wait(0)
        dot_f, dot_l = zero, zero
        for t in range(4):
            for where, outer in zip((part(t), part(t + 4)), unpacked(planes, 1 - colour, t)):
                full = src[where] + lat[where] * outer
                src[where] = full
                dot_f = dot_f + jnp.sum(full * first_g[where], axis=0)
                dot_l = dot_l + jnp.sum(full * last_g[where], axis=0)
        buffer = end_buffer(event)
        buffer[vert, 0] = dot_f
        buffer[vert, 1] = dot_l
        if event == 0:
            for i in range(4):
                buffer[vert, 2 + i] = own[i]
        rows_start(event, [dot_f, dot_l] + (own + [low0, up_top] if event == 0 else []))
        for peer in peers:
            end_copy(event, buffer, vert, peer).start()
        if event == 0:
            units_start(1)

        def forward(k, carry):
            f_l, f_u = carry
            j = top - k
            f_l = src[k] * inv[k] + fwd[k] * f_l
            f_u = src[j] * inv[j] + fwd[j] * f_u
            work[k] = f_l
            work[j] = f_u
            return f_l, f_u

        f_l, f_u = lax.fori_loop(0, half, forward, (zero, zero), unroll=True)
        y_l = (f_l + piv_l * f_u) * meet
        y_u = f_u + piv_u * y_l
        work[half - 1] = y_l
        work[half] = y_u

        def backward(i, carry):
            y_l, y_u = carry
            k = half - 1 - i
            j = half + i
            y_l = work[k] + bwd[k] * y_l
            y_u = work[j] + bwd[j] * y_u
            work[k] = y_l
            work[j] = y_u
            return y_l, y_u

        lax.fori_loop(1, half, backward, (y_l, y_u), unroll=True)
        if event > 0:
            acc = None
            for t in range(4):
                acc = packed(acc, work[part(t)], work[part(t + 4)], t, colour)
            halo_start(event + 1, acc)
        if event == 1:
            units_start(0)
        for peer in peers:
            end_copy(event, buffer, peer, peer).wait_recv()
        if event == 0:
            table = [[ends0[e, 2 + i] for i in range(4)] for e in range(depth)]
            interface_coefficients(table, own, low0, up_top, coef)
        from_b, from_a = zero, zero
        for n in range(2 * depth):
            value = buffer[n // 2, n % 2]
            from_b = from_b + coef[0, n] * value
            from_a = from_a + coef[1, n] * value
        reach[colour] = (from_b, from_a)
        old = guess if event == 0 else out
        acc = None
        for t in range(4):
            pair = []
            for where in (part(t), part(t + 4)):
                new = work[where] + first_g[where] * from_b + last_g[where] * from_a
                new = jnp.where(chosen[None], new, old[where])
                out[where] = new
                pair.append(new)
            if event == 0:
                acc = packed(acc, pair[0], pair[1], t, colour)
        if event == 0:
            halo_start(1, acc)
        if event == 2 * SWEEPS - 1:
            def keep_source(t, carry):
                at = pl.ds(pl.multiple_of(t * chunk, chunk), chunk)
                inner = rhs[at] + lat[at] * lateral_inner(out[at])
                src[at] = jnp.where(red[None], inner, src[at])
                return carry
            lax.fori_loop(0, 8, keep_source, 0, unroll=True)
        else:
            partial_source(out)
        rows_wait(event)
        if event == 0:
            table = [[row_item(0, e, 2 + i) for i in range(4)] for e in range(depth)]
            mine = [row_item(0, vert, 2 + i) for i in range(6)]
            interface_coefficients(table, mine[:4], mine[4], mine[5], row_coef)
            halo_wait(1)
            planes = halo.at[1]
            continue
        from_b, from_a = zero, zero
        for n in range(2 * depth):
            value = row_item(event, n // 2, n % 2)
            from_b = from_b + row_coef[0, n] * value
            from_a = from_a + row_coef[1, n] * value
        if event < 3:
            from_sides(lambda side: unit_copy(colour, side).wait_recv())
        halo_wait(event + 1)
        join_planes(event + 1, colour, from_b, from_a)
        planes = joined

    out_store = pltpu.make_async_copy(out, out_hbm, store_sem.at[0])
    out_store.start()
    from_b = jnp.where(red, reach[0][0], reach[1][0])
    from_a = jnp.where(red, reach[0][1], reach[1][1])

    def applied(k):
        low_k = low0 if k == 0 else up[k - 1]
        under = from_b if k == 0 else low_k * out[k - 1]
        over = from_a if k == top else up[k] * out[k + 1]
        return (4.0 * lat[k] + up[k] + low_k) * out[k] - over - under

    for t in range(4):
        for where, outer in zip((part(t), part(t + 4)), unpacked(joined, 1, t)):
            src[where] = src[where] + lat[where] * jnp.where(red[None], outer, 0.0)
    bottom_res = src[0] - applied(0)
    top_res = src[top] - applied(top)
    res[0] = bottom_res
    res[top] = top_res
    edge_out[0] = top_res
    edge_out[1] = bottom_res

    @pl.when(vert < depth - 1)
    def _():
        edge_copy(0).start()

    @pl.when(vert > 0)
    def _():
        edge_copy(1).start()

    def inner_level(k, carry):
        low_k, up_k = up[k - 1], up[k]
        res[k] = src[k] - (
            (4.0 * lat[k] + up_k + low_k) * out[k] - up_k * out[k + 1] - low_k * out[k - 1]
        )
        return carry

    lax.fori_loop(1, top, inner_level, 0, unroll=True)

    def restrict(m, carry):
        coarse[m] = (
            res[2 * m - 1] + 3.0 * res[2 * m] + 3.0 * res[2 * m + 1] + res[2 * m + 2]
        ) * 0.125
        return carry

    last = levels // 2 - 1
    lax.fori_loop(1, last, restrict, 0, unroll=True)

    def coarse_store(first, count, i):
        at = pl.ds(first, count)
        return pltpu.make_async_copy(coarse.at[at], coarse_hbm.at[at], store_sem.at[i])

    stores = [coarse_store(1, last - 1, 1), coarse_store(0, 1, 2), coarse_store(last, 1, 3)]
    stores[0].start()

    @pl.when(vert > 0)
    def _():
        edge_copy(0).wait_recv()

    @pl.when(vert < depth - 1)
    def _():
        edge_copy(1).wait_recv()

    coarse[0] = (edge_in[0] + 3.0 * res[0] + 3.0 * res[1] + res[2]) * 0.125
    coarse[last] = (res[top - 2] + 3.0 * res[top - 1] + 3.0 * res[top] + edge_in[1]) * 0.125

    stores[1].start()
    stores[2].start()

    @pl.when(vert < depth - 1)
    def _():
        low_copy().wait_send()
        edge_copy(0).wait_send()

    @pl.when(vert > 0)
    def _():
        edge_copy(1).wait_send()

    for event in range(2 * SWEEPS):
        for peer in peers:
            end_copy(event, end_buffer(event), vert, peer).wait_send()

        def sent(side):
            for peer in everyone:
                row_copy(event, side, vert, peer).wait_send()

        to_sides(sent)
    for colour in range(2):
        to_sides(lambda side: unit_copy(colour, side).wait_send())
    for event in range(2 * SWEEPS + 1):
        @pl.when(ha < width - 1)
        def _():
            halo_copy(event, 0).wait_send()

        @pl.when(ha > 0)
        def _():
            halo_copy(event, 1).wait_send()
    out_store.wait()
    for copy in stores:
        copy.wait()


def to_tiles(a):
    levels, rows, cols = a.shape
    return a.reshape(levels, rows, cols // LANES, LANES).transpose(0, 2, 1, 3).reshape(
        levels, rows * (cols // LANES), LANES
    )


def from_tiles(a, rows, cols):
    levels = a.shape[0]
    return a.reshape(levels, cols // LANES, rows, LANES).transpose(0, 2, 1, 3).reshape(
        levels, rows, cols
    )


def local(depth, width, rhs, guess, vertical_coupling, lateral_coupling):
    levels, rows, cols = guess.shape
    f32 = jnp.float32
    tile = (8, LANES)
    field = pltpu.VMEM((levels,) + tile, f32)
    events = 2 * SWEEPS + 1
    dma = pltpu.SemaphoreType.DMA
    smoothed, coarse = pl.pallas_call(
        functools.partial(kernel, depth, width),
        out_shape=(
            jax.ShapeDtypeStruct((levels,) + tile, f32),
            jax.ShapeDtypeStruct((levels // 2,) + tile, f32),
        ),
        in_specs=[pl.BlockSpec(memory_space=pl.ANY)] * 4,
        out_specs=(pl.BlockSpec(memory_space=pl.ANY),) * 2,
        scratch_shapes=[field, pltpu.VMEM((levels // 2,) + tile, f32)] + [field] * 12 + [
            pltpu.VMEM(tile, f32),
            pltpu.VMEM((events, 2, levels // 8) + tile, f32),
            pltpu.VMEM((events, 2, levels // 8) + tile, f32),
            pltpu.VMEM((depth, 6) + tile, f32),
            pltpu.VMEM((events - 2, depth, 2) + tile, f32),
            pltpu.VMEM((2, 2 * depth) + tile, f32),
            pltpu.VMEM((2,) + tile, f32),
            pltpu.VMEM((2,) + tile, f32),
            pltpu.VMEM((2, 2) + tile, f32),
            pltpu.VMEM((2, depth, 2) + tile, f32),
            pltpu.VMEM((events - 2, 2, 1) + tile, f32),
            pltpu.VMEM((events - 2, 2, depth, 1) + tile, f32),
            pltpu.VMEM((2, 2 * depth) + tile, f32),
            pltpu.VMEM((2, 2, 2, levels // 8) + tile, f32),
            pltpu.VMEM((2, 2, 2, levels // 8) + tile, f32),
            pltpu.VMEM((2, levels // 8) + tile, f32),
            dma, dma,
            dma((events, 2)), dma((events, 2)),
            dma((events - 1, depth)), dma((events - 1, depth)),
            dma((2,)), dma((2,)), dma((4,)), dma((4,)),
            dma((events - 1, 2, depth)), dma((events - 1, 2, depth)), dma((2, 2)), dma((2, 2)),
        ],
        compiler_params=pltpu.CompilerParams(
            collective_id=0, has_side_effects=True, vmem_limit_bytes=56 * 1024 * 1024
        ),
        cost_estimate=pl.CostEstimate(
            flops=200 * levels * rows * cols, bytes_accessed=22 * levels * rows * cols,
            transcendentals=0,
        ),
    )(*[to_tiles(a) for a in (rhs, guess, vertical_coupling, lateral_coupling)])
    return from_tiles(smoothed, rows, cols), from_tiles(coarse, rows, cols)


def solution(mesh):
    spec = P("vert", "ha", None)
    return jax.shard_map(
        functools.partial(local, mesh.shape["vert"], mesh.shape["ha"]),
        mesh=mesh,
        in_specs=(spec,) * 4,
        out_specs=(spec, spec),
        check_vma=False,
    )
```
